32 devices in a mesh: dp: 4 (over x, core), ctx: 8 (over z, y).
Axes of the slice: x: 2, y: 2, z: 4, core: 2. Of those that a mesh axis runs over, the one named last changes fastest.
Arguments:
- queries: bfloat16 [8192, 256], P(('dp', 'ctx')), parts along dimension 0, may hold values from -6 to 6
- keys: bfloat16 [8192, 256], P(('dp', 'ctx')), parts along dimension 0, may hold values from -6 to 6
- values: bfloat16 [8192, 256], P(('dp', 'ctx')), parts along dimension 0, may hold values from -6 to 6
- out_grad: bfloat16 [8192, 256], P(('dp', 'ctx')), parts along dimension 0, may hold values from -16 to 16
- block_list: int32 [64, 5], P(('dp', 'ctx')), parts along dimension 0, may hold values from -1 to 15, as said below
- causal: int32 [64], P(('dp', 'ctx')), parts along dimension 0, may hold values 0 or 1
Outputs:
- query_grad: bfloat16 [8192, 256], P(('dp', 'ctx')), parts along dimension 0
- key_grad: bfloat16 [8192, 256], P(('dp', 'ctx')), parts along dimension 0
- value_grad: bfloat16 [8192, 256], P(('dp', 'ctx')), parts along dimension 0
The draws below stay inside these ranges and needn't reach their ends.
There are 4 independent parts, one for each index of `dp`. The reference program is written for one: setup_inputs(seed, part) draws one part's arguments, and reference() takes and returns one part's arrays. A program takes and returns all parts, laid end to end along the dimension named above; each array names one. Nothing has to cross between parts.
Inputs may be any that keep to these rules, and one draw needn't show every extreme that they name: `block_list`: entry 0 of block b is b; entry j, for j from 1 to 4, is b - 2**(j-1) or -1, and is -1 where that would be negative.
All inputs are finite; a program needn't handle non-finite values. No bound on the sum of `causal` on one device may be relied on, other than what follows from the above.
Results may differ from the reference program's by a relative error of at most 0.034.
Values may be sent and summed in bfloat16 or wider, within the bound.
A program may use at most 64 MiB of HBM per device.

```python
import jax
import jax.numpy as jnp
from jax import lax

BLOCK = 128
HEADS = 2
HEAD_DIM = 128
SEQ = 2048
BPD = 2
NB = 16
LEVELS = 4
ENTRIES = 5


def drawn_pair(key):
    feat = HEADS * HEAD_DIM
    base_q = jnp.clip(jax.random.normal(jax.random.fold_in(key, 11), (SEQ, feat), jnp.float32), -6.0, 6.0)
    base_k = jnp.clip(jax.random.normal(jax.random.fold_in(key, 12), (SEQ, feat), jnp.float32), -6.0, 6.0)
    return (base_q, base_k)


def draw_queries(key, part):
    return drawn_pair(key)[0].astype(jnp.bfloat16)


def draw_keys(key, part):
    return drawn_pair(key)[1].astype(jnp.bfloat16)


def draw_block_list(key, part):
    block_ids = jnp.arange(NB, dtype=jnp.int32)
    reaches = jnp.left_shift(jnp.int32(1), jnp.arange(LEVELS, dtype=jnp.int32))
    target = block_ids[:, None] - reaches[None, :]
    keeper = jax.random.randint(jax.random.fold_in(key, 21), (NB, LEVELS), 0, 4) > 0
    listed = jnp.where((target >= 0) & keeper, target, -1).astype(jnp.int32)
    return jnp.concatenate([block_ids[:, None], listed], 1)


def place_ends(entries, stream_key, smallest, high):
    spot = [jax.random.randint(jax.random.fold_in(stream_key, axis), (), 0, length) for axis, length in enumerate(entries.shape)]
    longest = entries.shape.index(max(entries.shape))
    beside = spot[:longest] + [(spot[longest] + 1) % entries.shape[longest]] + spot[longest + 1:]
    return entries.at[tuple(spot)].set(smallest).at[tuple(beside)].set(high)


def levels(rng, extent, pieces, smallest, top_value):
    loudness = 1.0
    for dim, parts in pieces:
        heights = jax.random.uniform(jax.random.fold_in(jax.random.fold_in(rng, 6), dim), (parts,), jnp.float32, smallest / len(pieces), top_value / len(pieces))
        loudness = loudness * jnp.repeat(jnp.exp(heights), extent[dim] // parts).reshape((-1,) + (1,) * (len(extent) - 1 - dim))
    return loudness


def centred(stream_key, dims, scale, bound, pieces=(), held_as=jnp.bfloat16):
    entries = scale * jax.random.normal(stream_key, dims, jnp.float32)
    if pieces:
        entries = entries * levels(stream_key, dims, pieces, -0.22, 0.18)
    return jnp.clip(entries, -bound, bound).astype(held_as)


def setup_inputs(seed: int = 0, part: int = 0) -> dict:
    seeds = jax.random.split(jax.random.key(seed), 7)
    part_keys = jax.random.split(jax.random.fold_in(seeds[6], part), 7)
    queries = draw_queries(jax.random.fold_in(jax.random.fold_in(seeds[6], part), 71), part)
    keys = draw_keys(jax.random.fold_in(jax.random.fold_in(seeds[6], part), 71), part)
    values = centred(part_keys[2], (SEQ, HEADS * HEAD_DIM), 1.0, 6.0, ((0, 8),))
    out_grad = centred(part_keys[3], (SEQ, HEADS * HEAD_DIM), 4.0, 16.0, ((0, 8),))
    block_list = draw_block_list(jax.random.fold_in(jax.random.fold_in(seeds[6], part), 71), part)
    causal = place_ends((jax.random.randint(part_keys[5], (NB,), 0, 4) < 3).astype(jnp.int32), jax.random.fold_in(part_keys[5], 1), 0, 1)
    return dict(queries=queries, keys=keys, values=values, out_grad=out_grad, block_list=block_list, causal=causal)


def reference(queries, keys, values, out_grad, block_list, causal):
    feat = HEADS * HEAD_DIM
    scale = HEAD_DIM ** -0.5
    q_blocks = queries.reshape(NB, BLOCK, HEADS, HEAD_DIM)
    k_blocks = keys.reshape(NB, BLOCK, HEADS, HEAD_DIM)
    v_blocks = values.reshape(NB, BLOCK, HEADS, HEAD_DIM)
    g_blocks = out_grad.reshape(NB, BLOCK, HEADS, HEAD_DIM)
    positions = jnp.arange(BLOCK)
    lower = positions[:, None] >= positions[None, :]
    level_ids = jnp.arange(ENTRIES)

    def one_block(index):
        entry_row = block_list[index]
        valid = entry_row >= 0
        safe = jnp.maximum(entry_row, 0).astype(jnp.int32)
        key_set = k_blocks[safe].astype(jnp.float32)
        value_set = v_blocks[safe].astype(jnp.float32)
        query_here = q_blocks[index].astype(jnp.float32)
        grad_here = g_blocks[index].astype(jnp.float32)
        scores = jnp.einsum('thd,euhd->hteu', query_here, key_set) * scale
        self_mask = jnp.where(causal[index] > 0, lower, True)
        mask = jnp.where(level_ids[None, :, None] == 0, self_mask[:, None, :], True)
        mask = mask & valid[None, :, None]
        scores = jnp.where(mask[None], scores, -jnp.inf)
        top = jnp.max(scores, axis=(2, 3))
        lse = top + jnp.log(jnp.sum(jnp.exp(scores - top[:, :, None, None]), axis=(2, 3)))
        probs = jnp.exp(scores - lse[:, :, None, None])
        weights = probs.astype(jnp.bfloat16).astype(jnp.float32)
        dprobs = jnp.einsum('thd,euhd->hteu', grad_here, value_set)
        delta = jnp.sum(weights * dprobs, axis=(2, 3))
        dscores = (probs * (dprobs - delta[:, :, None, None])).astype(jnp.bfloat16).astype(jnp.float32)
        query_part = (jnp.einsum('hteu,euhd->thd', dscores, key_set) * scale).astype(jnp.bfloat16)
        key_part = jnp.einsum('hteu,thd->euhd', dscores, query_here) * scale
        value_part = jnp.einsum('hteu,thd->euhd', weights, grad_here)
        return (query_part.reshape(BLOCK, feat), key_part.reshape(ENTRIES, BLOCK, feat),
                value_part.reshape(ENTRIES, BLOCK, feat))

    query_grad, key_terms, value_terms = lax.map(one_block, jnp.arange(NB))

    def collect(terms):
        local_sum = terms[:, 0]
        near_sum = jnp.zeros((NB, BLOCK, feat), jnp.float32)
        far_sums = []
        block_ids = jnp.arange(NB)
        for level in range(1, ENTRIES):
            reach = 2 ** (level - 1)
            moved = jnp.concatenate([terms[reach:, level], jnp.zeros((reach, BLOCK, feat), jnp.float32)], 0)
            if reach <= BPD:
                remote = ((block_ids + reach) // BPD != block_ids // BPD)[:, None, None]
                local_sum = local_sum + jnp.where(remote, 0.0, moved)
                near_sum = near_sum + jnp.where(remote, moved, 0.0)
            else:
                far_sums.append(lax.optimization_barrier(moved.astype(jnp.bfloat16)).astype(jnp.float32))
        total = local_sum + lax.optimization_barrier(near_sum.astype(jnp.bfloat16)).astype(jnp.float32)
        for piece in far_sums:
            total = total + piece
        return total.reshape(SEQ, feat).astype(jnp.bfloat16)

    return query_grad.reshape(SEQ, feat), collect(key_terms), collect(value_terms)
```

```python
import functools

import jax
import jax.numpy as jnp
from jax import lax
from jax.experimental import pallas as pl
from jax.experimental.pallas import tpu as pltpu
from jax.sharding import PartitionSpec as P

BLOCK = 128
HEADS = 2
BPD = 2
LOG2E = 1.4426950408889634
BIG = 1e30
MESH = pl.DeviceIdType.MESH
F32 = jnp.float32
BF16 = jnp.bfloat16


def dot_nt(a, b):
    return lax.dot_general(a, b, (((1,), (1,)), ((), ())), preferred_element_type=F32)


def dot_nn(a, b):
    return lax.dot_general(a, b, (((1,), (0,)), ((), ())), preferred_element_type=F32)


def dot_tn(a, b):
    return lax.dot_general(a, b, (((0,), (0,)), ((), ())), preferred_element_type=F32)


def rows(b):
    return slice(b * BLOCK, (b + 1) * BLOCK)


def kernel(
    n, dists, bl, ca, q, k, v, g, dq, dk, dv,
    fbuf, bbuf, sout, sin, sq, dpq, sk, dpk,
    fsend, frecv, bsend, brecv, ssend, srecv,
):
    d = q.shape[1] // HEADS
    scale = d ** (-0.5)
    c2 = scale * LOG2E
    me = lax.axis_index("ctx")
    odd = lax.rem(me, 2) == 1
    even = lax.rem(me, 2) == 0
    chunks = [(i, r) for i in range(2) for r in range(BPD)]

    def cols(h):
        return slice(h * d, (h + 1) * d)

    barrier = pltpu.get_barrier_semaphore()
    for k_ in range(dists):
        for step in (2**k_, -(2**k_)):
            there = me + step

            @pl.when((there >= 0) & (there < n))
            def _():
                pl.semaphore_signal(barrier, inc=1, device_id={"ctx": there}, device_id_type=MESH)

    for k_ in range(dists):

        @pl.when(me < 2**k_)
        def _():
            fbuf[k_] = jnp.zeros(fbuf.shape[1:], BF16)

        @pl.when(me + 2**k_ >= n)
        def _():
            bbuf[k_] = jnp.zeros(bbuf.shape[1:], BF16)
            sin[k_] = jnp.full(sin.shape[1:], BIG, F32)

    peers = 0
    for k_ in range(dists):
        for step in (2**k_, -(2**k_)):
            there = me + step
            peers = peers + jnp.where((there >= 0) & (there < n), 1, 0)
    pl.semaphore_wait(barrier, peers)

    def own(pair):
        return lambda i, r: pair[i].at[pl.ds(r * BLOCK, BLOCK)]

    def held(buf, level):
        return lambda i, r: buf.at[level, i, pl.ds(r * BLOCK, BLOCK)]

    def copy(src, buf, level, chunk, send, recv, there):
        i, r = chunks[chunk]
        return pltpu.make_async_remote_copy(
            src_ref=src(i, r),
            dst_ref=buf.at[level, i, pl.ds(r * BLOCK, BLOCK)],
            send_sem=send.at[level, chunk],
            recv_sem=recv.at[level, chunk],
            device_id={"ctx": there},
            device_id_type=MESH,
        )

    def fcopy(src, level, chunk, there):
        return copy(src, fbuf, level, chunk, fsend, frecv, there)

    def bcopy(src, level, chunk, there):
        return copy(src, bbuf, level, chunk, bsend, brecv, there)

    own_kv, own_qg = own((k, v)), own((q, g))
    near_kv, near_qg = held(fbuf, 1), held(bbuf, 1)
    count = len(chunks)

    for c in range(count):

        @pl.when(me + 2 < n)
        def _():
            fcopy(own_kv, 1, c, me + 2).start()

        @pl.when(me >= 2)
        def _():
            bcopy(own_qg, 1, c, me - 2).start()

    for c in range(count):

        @pl.when(even)
        def _():
            fcopy(own_kv, 0, c, me + 1).start()

        @pl.when(odd)
        def _():
            bcopy(own_qg, 0, c, me - 1).start()

    def relay(level):
        step = 2**level
        for c in range(count):

            @pl.when(me >= step)
            def _():
                fcopy(own_kv, level, c, me - step).wait_recv()

                if 1 <= level < dists - 1:

                    @pl.when(me + step < n)
                    def _():
                        fcopy(held(fbuf, level), level + 1, c, me + step).start()

                if level == 1:

                    @pl.when(odd)
                    def _():
                        fcopy(near_kv, 0, c, me - 1).start()

            @pl.when(me + step < n)
            def _():
                bcopy(own_qg, level, c, me + step).wait_recv()

                if 1 <= level < dists - 1:

                    @pl.when(me >= step)
                    def _():
                        bcopy(held(bbuf, level), level + 1, c, me - step).start()

                if level == 1:

                    @pl.when(even)
                    def _():
                        bcopy(near_qg, 0, c, me + 1).start()

    stats = {}

    def bias(b, level):
        return jnp.where(bl[b, level] >= 0, 0.0, -BIG).astype(F32)

    def query_tile(b, h, level, kb, vb):
        s = dot_nt(kb, q[rows(b), cols(h)]) * c2
        if level == 0:
            uu = lax.broadcasted_iota(jnp.int32, (BLOCK, BLOCK), 0)
            tt = lax.broadcasted_iota(jnp.int32, (BLOCK, BLOCK), 1)
            s = jnp.where((uu - tt) * ca[b] > 0, -BIG, s)
        else:
            s = s + bias(b, level)
        dp = dot_nt(vb, g[rows(b), cols(h)])
        sq[b, h, level] = s
        dpq[b, h, level] = dp
        top = jnp.max(s, axis=0, keepdims=True)
        if (b, h) not in stats:
            e = jnp.exp2(s - top)
            stats[b, h] = (
                top, jnp.sum(e, axis=0, keepdims=True), jnp.sum(e * dp, axis=0, keepdims=True)
            )
        else:
            m, l, w = stats[b, h]
            new = jnp.maximum(m, top)
            a = jnp.exp2(m - new)
            e = jnp.exp2(s - new)
            stats[b, h] = (
                new,
                l * a + jnp.sum(e, axis=0, keepdims=True),
                w * a + jnp.sum(e * dp, axis=0, keepdims=True),
            )

    def far_tiles(level):
        tiles = [(0, 0, 0), (1, 1, HEADS)]
        if level == 0:
            tiles.append((0, 1, 4 * HEADS))
        return tiles

    def key_tile(level, slot, qb, kb, h):
        sk[level, slot, h] = dot_nt(k[rows(kb), cols(h)], bbuf[level, 0, rows(qb), cols(h)]) * c2
        dpk[level, slot, h] = dot_nt(v[rows(kb), cols(h)], bbuf[level, 1, rows(qb), cols(h)])

    def query_level(level):
        for h in range(HEADS):
            if level == 0:
                query_tile(0, h, 1, fbuf[0, 0, rows(1), cols(h)], fbuf[0, 1, rows(1), cols(h)])
            for b in range(BPD):
                query_tile(
                    b, h, level + 2,
                    fbuf[level, 0, rows(b), cols(h)], fbuf[level, 1, rows(b), cols(h)],
                )

    def key_level(level):
        for slot, (qb, kb, _) in enumerate(far_tiles(level)):
            for h in range(HEADS):
                key_tile(level, slot, qb, kb, h)

    for h in range(HEADS):
        for b in range(BPD):
            query_tile(b, h, 0, k[rows(b), cols(h)], v[rows(b), cols(h)])
        query_tile(1, h, 1, k[rows(0), cols(h)], v[rows(0), cols(h)])

    relay(1)
    query_level(1)
    key_level(1)
    for level in [0] + list(range(2, dists)):
        relay(level)
        query_level(level)
        if level < dists - 1:
            key_level(level)

    final = {}
    for b in range(BPD):
        for h in range(HEADS):
            m, l, w = stats[b, h]
            final[b, h] = (m + jnp.log2(l), w / l)
    for level in range(dists):
        for b in range(BPD):
            for h in range(HEADS):
                lse, delta = final[b, h]
                row = b * HEADS + h
                sout[level, row : row + 1] = lse - bias(b, level + 2)
                row = row + BPD * HEADS
                sout[level, row : row + 1] = delta
                row = row + BPD * HEADS
                first = lse - bias(b, 1)
                sout[level, row : row + 1] = first

    def scopy(level, there):
        return pltpu.make_async_remote_copy(
            src_ref=sout.at[level],
            dst_ref=sin.at[level],
            send_sem=ssend.at[level],
            recv_sem=srecv.at[level],
            device_id={"ctx": there},
            device_id_type=MESH,
        )

    for level in range(dists - 1, -1, -1):

        @pl.when(me >= 2**level)
        def _():
            scopy(level, me - 2**level).start()

    key_level(dists - 1)

    dk_acc, dv_acc = {}, {}

    def add(acc, at, term):
        acc[at] = acc[at] + term if at in acc else term

    entries = bl.shape[1]
    for b in range(BPD):
        for h in range(HEADS):
            lse, delta = final[b, h]
            total = None
            for level in range(entries):
                p = jnp.exp2(sq[b, h, level] - lse)
                ds = (p * (dpq[b, h, level] - delta)).astype(BF16)
                if level == 0:
                    kb, local = k[rows(b), cols(h)], b
                elif level == 1 and b == 1:
                    kb, local = k[rows(0), cols(h)], 0
                elif level == 1:
                    kb, local = fbuf[0, 0, rows(1), cols(h)], None
                else:
                    kb, local = fbuf[level - 2, 0, rows(b), cols(h)], None
                term = dot_tn(ds, kb)
                total = term if total is None else total + term
                if local is not None:
                    add(dk_acc, (local, h), dot_nn(ds, q[rows(b), cols(h)]))
                    add(dv_acc, (local, h), dot_nn(p.astype(BF16), g[rows(b), cols(h)]))
            dq[rows(b), cols(h)] = (total * scale).astype(BF16)

    for level in range(dists):

        @pl.when(me + 2**level < n)
        def _():
            scopy(level, me + 2**level).wait_recv()

    for level in range(dists):
        for slot, (qb, kb, lse_row) in enumerate(far_tiles(level)):
            for h in range(HEADS):
                lse = sin[level, lse_row + h : lse_row + h + 1]
                at = (BPD + qb) * HEADS + h
                delta = sin[level, at : at + 1]
                p = jnp.exp2(sk[level, slot, h] - lse)
                ds = (p * (dpk[level, slot, h] - delta)).astype(BF16)
                add(dk_acc, (kb, h), dot_nn(ds, bbuf[level, 0, rows(qb), cols(h)]))
                add(dv_acc, (kb, h), dot_nn(p.astype(BF16), bbuf[level, 1, rows(qb), cols(h)]))
    for b in range(BPD):
        for h in range(HEADS):
            dk[rows(b), cols(h)] = (dk_acc[b, h] * scale).astype(BF16)
            dv[rows(b), cols(h)] = dv_acc[b, h].astype(BF16)

    for c in range(count):

        @pl.when(me + 2 < n)
        def _():
            fcopy(own_kv, 1, c, me + 2).wait_send()

        @pl.when(me >= 2)
        def _():
            bcopy(own_qg, 1, c, me - 2).wait_send()

        @pl.when(even)
        def _():
            fcopy(own_kv, 0, c, me + 1).wait_send()

            @pl.when(me + 2 < n)
            def _():
                bcopy(near_qg, 0, c, me + 1).wait_send()

        @pl.when(odd)
        def _():
            bcopy(own_qg, 0, c, me - 1).wait_send()

            @pl.when(me >= 2)
            def _():
                fcopy(near_kv, 0, c, me - 1).wait_send()

        for level in range(1, dists - 1):
            step = 2**level

            @pl.when((me >= step) & (me + step < n))
            def _():
                fcopy(held(fbuf, level), level + 1, c, me + step).wait_send()
                bcopy(held(bbuf, level), level + 1, c, me - step).wait_send()

    for level in range(dists):

        @pl.when(me >= 2**level)
        def _():
            scopy(level, me - 2**level).wait_send()


def on_device(n, queries, keys, values, out_grad, block_list, causal):
    tok, feat = queries.shape
    entries = block_list.shape[1]
    dists = entries - 2
    d = feat // HEADS
    vmem = pl.BlockSpec(memory_space=pltpu.VMEM)
    smem = pl.BlockSpec(memory_space=pltpu.SMEM)
    chunks = 2 * BPD
    tile = (BLOCK, BLOCK)
    sems = pltpu.SemaphoreType.DMA((dists, chunks))
    out = jax.ShapeDtypeStruct((tok, feat), BF16)
    return pl.pallas_call(
        functools.partial(kernel, n, dists),
        out_shape=(out, out, out),
        in_specs=[smem, smem, vmem, vmem, vmem, vmem],
        out_specs=(vmem, vmem, vmem),
        scratch_shapes=[
            pltpu.VMEM((dists, 2, tok, feat), BF16),
            pltpu.VMEM((dists, 2, tok, feat), BF16),
            pltpu.VMEM((dists, 16, BLOCK), F32),
            pltpu.VMEM((dists, 16, BLOCK), F32),
            pltpu.VMEM((BPD, HEADS, entries) + tile, F32),
            pltpu.VMEM((BPD, HEADS, entries) + tile, F32),
            pltpu.VMEM((dists, 3, HEADS) + tile, F32),
            pltpu.VMEM((dists, 3, HEADS) + tile, F32),
            sems, sems, sems, sems,
            pltpu.SemaphoreType.DMA((dists,)),
            pltpu.SemaphoreType.DMA((dists,)),
        ],
        compiler_params=pltpu.CompilerParams(
            collective_id=0, has_side_effects=True, vmem_limit_bytes=48 * 2**20
        ),
        cost_estimate=pl.CostEstimate(
            flops=128 * 2 * BLOCK * BLOCK * d, bytes_accessed=7 * tok * feat * 2,
            transcendentals=54 * BLOCK * BLOCK,
        ),
    )(block_list, causal, queries, keys, values, out_grad)


def solution(mesh):
    rowspec = P(("dp", "ctx"), None)
    return jax.shard_map(
        functools.partial(on_device, mesh.shape["ctx"]),
        mesh=mesh,
        in_specs=(rowspec,) * 5 + (P(("dp", "ctx")),),
        out_specs=(rowspec,) * 3,
        check_vma=False,
    )
```

```python
import functools

import jax
import jax.numpy as jnp
from jax import lax
from jax.experimental import pallas as pl
from jax.experimental.pallas import tpu as pltpu
from jax.sharding import PartitionSpec as P

BLOCK = 128
HEADS = 2
BPD = 2
LOG2E = 1.4426950408889634
BIG = 1e30
MESH = pl.DeviceIdType.MESH
F32 = jnp.float32
BF16 = jnp.bfloat16


def dot_nt(a, b):
    return lax.dot_general(a, b, (((1,), (1,)), ((), ())), preferred_element_type=F32)


def dot_nn(a, b):
    return lax.dot_general(a, b, (((1,), (0,)), ((), ())), preferred_element_type=F32)


def dot_tn(a, b):
    return lax.dot_general(a, b, (((0,), (0,)), ((), ())), preferred_element_type=F32)


def rows(b):
    return slice(b * BLOCK, (b + 1) * BLOCK)


def kernel(
    n, dists, bl_hbm, ca_hbm, q_hbm, k_hbm, v_hbm, g_hbm, dq, dk, dv,
    bl, ca, q, k, v, g, fbuf, bbuf, sout, sin, sq, dpq, sk, dpk,
    fsend, frecv, bsend, brecv, ssend, srecv, isem,
):
    d = q.shape[1] // HEADS
    scale = d ** (-0.5)
    c2 = scale * LOG2E
    me = lax.axis_index("ctx")
    odd = lax.rem(me, 2) == 1
    even = lax.rem(me, 2) == 0
    chunks = [(i, r) for i in range(2) for r in range(BPD)]

    def cols(h):
        return slice(h * d, (h + 1) * d)

    fetches = [
        pltpu.make_async_copy(src, dst, isem.at[at])
        for at, (src, dst) in enumerate(
            [(k_hbm, k), (q_hbm, q), (v_hbm, v), (g_hbm, g), (bl_hbm, bl), (ca_hbm, ca)]
        )
    ]
    for fetch in fetches:
        fetch.start()

    barrier = pltpu.get_barrier_semaphore()
    for k_ in range(dists):
        for step in (2**k_, -(2**k_)):
            there = me + step

            @pl.when((there >= 0) & (there < n))
            def _():
                pl.semaphore_signal(barrier, inc=1, device_id={"ctx": there}, device_id_type=MESH)

    for k_ in range(dists):

        @pl.when(me < 2**k_)
        def _():
            fbuf[k_] = jnp.zeros(fbuf.shape[1:], BF16)

        @pl.when(me + 2**k_ >= n)
        def _():
            bbuf[k_] = jnp.zeros(bbuf.shape[1:], BF16)
            sin[k_] = jnp.full(sin.shape[1:], BIG, F32)

    peers = 0
    for k_ in range(dists):
        for step in (2**k_, -(2**k_)):
            there = me + step
            peers = peers + jnp.where((there >= 0) & (there < n), 1, 0)
    pl.semaphore_wait(barrier, peers)
    for fetch in fetches:
        fetch.wait()

    def own(pair):
        return lambda i, r: pair[i].at[pl.ds(r * BLOCK, BLOCK)]

    def held(buf, level):
        return lambda i, r: buf.at[level, i, pl.ds(r * BLOCK, BLOCK)]

    def copy(src, buf, level, chunk, send, recv, there):
        i, r = chunks[chunk]
        return pltpu.make_async_remote_copy(
            src_ref=src(i, r),
            dst_ref=buf.at[level, i, pl.ds(r * BLOCK, BLOCK)],
            send_sem=send.at[level, chunk],
            recv_sem=recv.at[level, chunk],
            device_id={"ctx": there},
            device_id_type=MESH,
        )

    def fcopy(src, level, chunk, there):
        return copy(src, fbuf, level, chunk, fsend, frecv, there)

    def bcopy(src, level, chunk, there):
        return copy(src, bbuf, level, chunk, bsend, brecv, there)

    own_kv, own_qg = own((k, v)), own((q, g))
    near_kv, near_qg = held(fbuf, 1), held(bbuf, 1)
    count = len(chunks)

    for c in range(count):

        @pl.when(me + 2 < n)
        def _():
            fcopy(own_kv, 1, c, me + 2).start()

        @pl.when(me >= 2)
        def _():
            bcopy(own_qg, 1, c, me - 2).start()

    for c in range(count):

        @pl.when(even)
        def _():
            fcopy(own_kv, 0, c, me + 1).start()

        @pl.when(odd)
        def _():
            bcopy(own_qg, 0, c, me - 1).start()

    def relay(level):
        step = 2**level
        for c in range(count):

            @pl.when(me >= step)
            def _():
                fcopy(own_kv, level, c, me - step).wait_recv()

                if 1 <= level < dists - 1:

                    @pl.when(me + step < n)
                    def _():
                        fcopy(held(fbuf, level), level + 1, c, me + step).start()

                if level == 1:

                    @pl.when(odd)
                    def _():
                        fcopy(near_kv, 0, c, me - 1).start()

            @pl.when(me + step < n)
            def _():
                bcopy(own_qg, level, c, me + step).wait_recv()

                if 1 <= level < dists - 1:

                    @pl.when(me >= step)
                    def _():
                        bcopy(held(bbuf, level), level + 1, c, me - step).start()

                if level == 1:

                    @pl.when(even)
                    def _():
                        bcopy(near_qg, 0, c, me + 1).start()

    stats = {}

    def bias(b, level):
        return jnp.where(bl[b, level] >= 0, 0.0, -BIG).astype(F32)

    def query_tile(b, h, level, kb, vb):
        s = dot_nt(kb, q[rows(b), cols(h)]) * c2
        if level == 0:
            uu = lax.broadcasted_iota(jnp.int32, (BLOCK, BLOCK), 0)
            tt = lax.broadcasted_iota(jnp.int32, (BLOCK, BLOCK), 1)
            s = jnp.where((uu - tt) * ca[b] > 0, -BIG, s)
        else:
            s = s + bias(b, level)
        dp = dot_nt(vb, g[rows(b), cols(h)])
        sq[b, h, level] = s
        dpq[b, h, level] = dp
        top = jnp.max(s, axis=0, keepdims=True)
        if (b, h) not in stats:
            e = jnp.exp2(s - top)
            stats[b, h] = (
                top, jnp.sum(e, axis=0, keepdims=True), jnp.sum(e * dp, axis=0, keepdims=True)
            )
        else:
            m, l, w = stats[b, h]
            new = jnp.maximum(m, top)
            a = jnp.exp2(m - new)
            e = jnp.exp2(s - new)
            stats[b, h] = (
                new,
                l * a + jnp.sum(e, axis=0, keepdims=True),
                w * a + jnp.sum(e * dp, axis=0, keepdims=True),
            )

    def far_tiles(level):
        tiles = [(0, 0, 0), (1, 1, HEADS)]
        if level == 0:
            tiles.append((0, 1, 4 * HEADS))
        return tiles

    def key_tile(level, slot, qb, kb, h):
        sk[level, slot, h] = dot_nt(k[rows(kb), cols(h)], bbuf[level, 0, rows(qb), cols(h)]) * c2
        dpk[level, slot, h] = dot_nt(v[rows(kb), cols(h)], bbuf[level, 1, rows(qb), cols(h)])

    def query_level(level):
        for h in range(HEADS):
            if level == 0:
                query_tile(0, h, 1, fbuf[0, 0, rows(1), cols(h)], fbuf[0, 1, rows(1), cols(h)])
            for b in range(BPD):
                query_tile(
                    b, h, level + 2,
                    fbuf[level, 0, rows(b), cols(h)], fbuf[level, 1, rows(b), cols(h)],
                )

    def key_level(level):
        for slot, (qb, kb, _) in enumerate(far_tiles(level)):
            for h in range(HEADS):
                key_tile(level, slot, qb, kb, h)

    for h in range(HEADS):
        for b in range(BPD):
            query_tile(b, h, 0, k[rows(b), cols(h)], v[rows(b), cols(h)])
        query_tile(1, h, 1, k[rows(0), cols(h)], v[rows(0), cols(h)])

    relay(1)
    query_level(1)
    key_level(1)
    for level in [0] + list(range(2, dists)):
        relay(level)
        query_level(level)
        if level < dists - 1:
            key_level(level)

    final = {}
    for b in range(BPD):
        for h in range(HEADS):
            m, l, w = stats[b, h]
            final[b, h] = (m + jnp.log2(l), w / l)
    for level in range(dists):
        for b in range(BPD):
            for h in range(HEADS):
                lse, delta = final[b, h]
                row = b * HEADS + h
                sout[level, row : row + 1] = lse - bias(b, level + 2)
                row = row + BPD * HEADS
                sout[level, row : row + 1] = delta
                row = row + BPD * HEADS
                first = lse - bias(b, 1)
                sout[level, row : row + 1] = first

    def scopy(level, there):
        return pltpu.make_async_remote_copy(
            src_ref=sout.at[level],
            dst_ref=sin.at[level],
            send_sem=ssend.at[level],
            recv_sem=srecv.at[level],
            device_id={"ctx": there},
            device_id_type=MESH,
        )

    for level in range(dists - 1, -1, -1):

        @pl.when(me >= 2**level)
        def _():
            scopy(level, me - 2**level).start()

    key_level(dists - 1)

    dk_acc, dv_acc = {}, {}

    def add(acc, at, term):
        acc[at] = acc[at] + term if at in acc else term

    entries = bl.shape[1]
    for b in range(BPD):
        for h in range(HEADS):
            lse, delta = final[b, h]
            total = None
            for level in range(entries):
                p = jnp.exp2(sq[b, h, level] - lse)
                ds = (p * (dpq[b, h, level] - delta)).astype(BF16)
                if level == 0:
                    kb, local = k[rows(b), cols(h)], b
                elif level == 1 and b == 1:
                    kb, local = k[rows(0), cols(h)], 0
                elif level == 1:
                    kb, local = fbuf[0, 0, rows(1), cols(h)], None
                else:
                    kb, local = fbuf[level - 2, 0, rows(b), cols(h)], None
                term = dot_tn(ds, kb)
                total = term if total is None else total + term
                if local is not None:
                    add(dk_acc, (local, h), dot_nn(ds, q[rows(b), cols(h)]))
                    add(dv_acc, (local, h), dot_nn(p.astype(BF16), g[rows(b), cols(h)]))
            dq[rows(b), cols(h)] = (total * scale).astype(BF16)

    for level in range(dists):

        @pl.when(me + 2**level < n)
        def _():
            scopy(level, me + 2**level).wait_recv()

    for level in range(dists):
        for slot, (qb, kb, lse_row) in enumerate(far_tiles(level)):
            for h in range(HEADS):
                lse = sin[level, lse_row + h : lse_row + h + 1]
                at = (BPD + qb) * HEADS + h
                delta = sin[level, at : at + 1]
                p = jnp.exp2(sk[level, slot, h] - lse)
                ds = (p * (dpk[level, slot, h] - delta)).astype(BF16)
                add(dk_acc, (kb, h), dot_nn(ds, bbuf[level, 0, rows(qb), cols(h)]))
                add(dv_acc, (kb, h), dot_nn(p.astype(BF16), bbuf[level, 1, rows(qb), cols(h)]))
    for b in range(BPD):
        for h in range(HEADS):
            dk[rows(b), cols(h)] = (dk_acc[b, h] * scale).astype(BF16)
            dv[rows(b), cols(h)] = dv_acc[b, h].astype(BF16)

    for c in range(count):

        @pl.when(me + 2 < n)
        def _():
            fcopy(own_kv, 1, c, me + 2).wait_send()

        @pl.when(me >= 2)
        def _():
            bcopy(own_qg, 1, c, me - 2).wait_send()

        @pl.when(even)
        def _():
            fcopy(own_kv, 0, c, me + 1).wait_send()

            @pl.when(me + 2 < n)
            def _():
                bcopy(near_qg, 0, c, me + 1).wait_send()

        @pl.when(odd)
        def _():
            bcopy(own_qg, 0, c, me - 1).wait_send()

            @pl.when(me >= 2)
            def _():
                fcopy(near_kv, 0, c, me - 1).wait_send()

        for level in range(1, dists - 1):
            step = 2**level

            @pl.when((me >= step) & (me + step < n))
            def _():
                fcopy(held(fbuf, level), level + 1, c, me + step).wait_send()
                bcopy(held(bbuf, level), level + 1, c, me - step).wait_send()

    for level in range(dists):

        @pl.when(me >= 2**level)
        def _():
            scopy(level, me - 2**level).wait_send()


def store(a, b, c, a_out, b_out, c_out, sem):
    copies = [
        pltpu.make_async_copy(src, dst, sem.at[at])
        for at, (src, dst) in enumerate([(a, a_out), (b, b_out), (c, c_out)])
    ]
    for copy in copies:
        copy.start()
    for copy in copies:
        copy.wait()


def on_device(n, queries, keys, values, out_grad, block_list, causal):
    tok, feat = queries.shape
    entries = block_list.shape[1]
    dists = entries - 2
    d = feat // HEADS
    vmem = pl.BlockSpec(memory_space=pltpu.VMEM)
    hbm = pl.BlockSpec(memory_space=pltpu.HBM)
    chunks = 2 * BPD
    tile = (BLOCK, BLOCK)
    sems = pltpu.SemaphoreType.DMA((dists, chunks))
    out = jax.ShapeDtypeStruct((tok, feat), BF16)
    grads = pl.pallas_call(
        functools.partial(kernel, n, dists),
        out_shape=(out, out, out),
        in_specs=[hbm] * 6,
        out_specs=(vmem, vmem, vmem),
        scratch_shapes=[
            pltpu.SMEM(block_list.shape, jnp.int32),
            pltpu.SMEM(causal.shape, jnp.int32),
            *[pltpu.VMEM((tok, feat), BF16)] * 4,
            pltpu.VMEM((dists, 2, tok, feat), BF16),
            pltpu.VMEM((dists, 2, tok, feat), BF16),
            pltpu.VMEM((dists, 16, BLOCK), F32),
            pltpu.VMEM((dists, 16, BLOCK), F32),
            pltpu.VMEM((BPD, HEADS, entries) + tile, F32),
            pltpu.VMEM((BPD, HEADS, entries) + tile, F32),
            pltpu.VMEM((dists, 3, HEADS) + tile, F32),
            pltpu.VMEM((dists, 3, HEADS) + tile, F32),
            sems, sems, sems, sems,
            pltpu.SemaphoreType.DMA((dists,)),
            pltpu.SemaphoreType.DMA((dists,)),
            pltpu.SemaphoreType.DMA((6,)),
        ],
        compiler_params=pltpu.CompilerParams(
            collective_id=0, has_side_effects=True, vmem_limit_bytes=63 * 2**20
        ),
        cost_estimate=pl.CostEstimate(
            flops=128 * 2 * BLOCK * BLOCK * d, bytes_accessed=7 * tok * feat * 2,
            transcendentals=54 * BLOCK * BLOCK,
        ),
    )(block_list, causal, queries, keys, values, out_grad)
    return pl.pallas_call(
        store,
        out_shape=(out, out, out),
        in_specs=[vmem] * 3,
        out_specs=(hbm, hbm, hbm),
        scratch_shapes=[pltpu.SemaphoreType.DMA((3,))],
        cost_estimate=pl.CostEstimate(
            flops=0, bytes_accessed=3 * tok * feat * 2, transcendentals=0
        ),
    )(*grads)


def solution(mesh):
    rowspec = P(("dp", "ctx"), None)
    return jax.shard_map(
        functools.partial(on_device, mesh.shape["ctx"]),
        mesh=mesh,
        in_specs=(rowspec,) * 5 + (P(("dp", "ctx")),),
        out_specs=(rowspec,) * 3,
        check_vma=False,
    )
```

```python
import functools

import jax
import jax.numpy as jnp
from jax import lax
from jax.experimental import pallas as pl
from jax.experimental.pallas import tpu as pltpu
from jax.sharding import PartitionSpec as P

BLOCK = 128
HEADS = 2
BPD = 2
LOG2E = 1.4426950408889634
BIG = 1e30
MESH = pl.DeviceIdType.MESH
F32 = jnp.float32
BF16 = jnp.bfloat16


def dot_nt(a, b):
    return lax.dot_general(a, b, (((1,), (1,)), ((), ())), preferred_element_type=F32)


def dot_nn(a, b):
    return lax.dot_general(a, b, (((1,), (0,)), ((), ())), preferred_element_type=F32)


def dot_tn(a, b):
    return lax.dot_general(a, b, (((0,), (0,)), ((), ())), preferred_element_type=F32)


def rows(b):
    return slice(b * BLOCK, (b + 1) * BLOCK)


def kernel(
    n, dists, bl_hbm, ca_hbm, q_hbm, k_hbm, v_hbm, g_hbm, dq, dk, dv,
    bl, ca, q, k, v, g, fbuf, bbuf, sout, sin, sq, dpq, sk, dpk,
    fsend, frecv, bsend, brecv, ssend, srecv, isem,
):
    d = q.shape[1] // HEADS
    scale = d ** (-0.5)
    c2 = scale * LOG2E
    me = lax.axis_index("ctx")
    odd = lax.rem(me, 2) == 1
    even = lax.rem(me, 2) == 0
    chunks = [(i, r) for i in range(2) for r in range(BPD)]

    def cols(h):
        return slice(h * d, (h + 1) * d)

    fetches = [
        pltpu.make_async_copy(src, dst, isem.at[at])
        for at, (src, dst) in enumerate(
            [(k_hbm, k), (q_hbm, q), (v_hbm, v), (g_hbm, g), (bl_hbm, bl), (ca_hbm, ca)]
        )
    ]
    for fetch in fetches:
        fetch.start()

    barrier = pltpu.get_barrier_semaphore()
    for k_ in range(dists):
        for step in (2**k_, -(2**k_)):
            there = me + step

            @pl.when((there >= 0) & (there < n))
            def _():
                pl.semaphore_signal(barrier, inc=1, device_id={"ctx": there}, device_id_type=MESH)

    for k_ in range(dists):

        @pl.when(me < 2**k_)
        def _():
            fbuf[k_] = jnp.zeros(fbuf.shape[1:], BF16)

        @pl.when(me + 2**k_ >= n)
        def _():
            bbuf[k_] = jnp.zeros(bbuf.shape[1:], BF16)
            sin[k_] = jnp.full(sin.shape[1:], BIG, F32)

    peers = 0
    for k_ in range(dists):
        for step in (2**k_, -(2**k_)):
            there = me + step
            peers = peers + jnp.where((there >= 0) & (there < n), 1, 0)
    pl.semaphore_wait(barrier, peers)
    for fetch in fetches:
        fetch.wait()

    def own(pair):
        return lambda i, r: pair[i].at[pl.ds(r * BLOCK, BLOCK)]

    def held(buf, level):
        return lambda i, r: buf.at[level, i, pl.ds(r * BLOCK, BLOCK)]

    def copy(src, buf, level, chunk, send, recv, there):
        i, r = chunks[chunk]
        return pltpu.make_async_remote_copy(
            src_ref=src(i, r),
            dst_ref=buf.at[level, i, pl.ds(r * BLOCK, BLOCK)],
            send_sem=send.at[level, chunk],
            recv_sem=recv.at[level, chunk],
            device_id={"ctx": there},
            device_id_type=MESH,
        )

    def fcopy(src, level, chunk, there):
        return copy(src, fbuf, level, chunk, fsend, frecv, there)

    def bcopy(src, level, chunk, there):
        return copy(src, bbuf, level, chunk, bsend, brecv, there)

    own_kv, own_qg = own((k, v)), own((q, g))
    near_kv, near_qg = held(fbuf, 1), held(bbuf, 1)
    count = len(chunks)

    for c in range(count):

        @pl.when(me + 2 < n)
        def _():
            fcopy(own_kv, 1, c, me + 2).start()

        @pl.when(me >= 2)
        def _():
            bcopy(own_qg, 1, c, me - 2).start()

    for c in range(count):

        @pl.when(even)
        def _():
            fcopy(own_kv, 0, c, me + 1).start()

        @pl.when(odd)
        def _():
            bcopy(own_qg, 0, c, me - 1).start()

    def arrive(level, which=range(count)):
        arrive_front(level, which)
        arrive_back(level, which)

    def arrive_front(level, which=range(count)):
        step = 2**level
        for c in which:

            @pl.when(me >= step)
            def _():
                fcopy(own_kv, level, c, me - step).wait_recv()

    def arrive_back(level, which=range(count)):
        step = 2**level
        for c in which:

            @pl.when(me + step < n)
            def _():
                bcopy(own_qg, level, c, me + step).wait_recv()

    def relay(level, which=range(count)):
        step = 2**level
        for c in which:

            @pl.when(me >= step)
            def _():

                if 1 <= level < dists - 1:

                    @pl.when(me + step < n)
                    def _():
                        fcopy(held(fbuf, level), level + 1, c, me + step).start()

                if level == 1:

                    @pl.when(odd)
                    def _():
                        fcopy(near_kv, 0, c, me - 1).start()

            @pl.when(me + step < n)
            def _():
                if 1 <= level < dists - 1:

                    @pl.when(me >= step)
                    def _():
                        bcopy(held(bbuf, level), level + 1, c, me - step).start()

                if level == 1:

                    @pl.when(even)
                    def _():
                        bcopy(near_qg, 0, c, me + 1).start()

    stats = {}

    def bias(b, level):
        return jnp.where(bl[b, level] >= 0, 0.0, -BIG).astype(F32)

    def query_tile(b, h, level, kb, vb):
        s = dot_nt(kb, q[rows(b), cols(h)]) * c2
        if level == 0:
            uu = lax.broadcasted_iota(jnp.int32, (BLOCK, BLOCK), 0)
            tt = lax.broadcasted_iota(jnp.int32, (BLOCK, BLOCK), 1)
            s = jnp.where((uu - tt) * ca[b] > 0, -BIG, s)
        else:
            s = s + bias(b, level)
        dp = dot_nt(vb, g[rows(b), cols(h)])
        sq[b, h, level] = s
        dpq[b, h, level] = dp
        top = jnp.max(s, axis=0, keepdims=True)
        if (b, h) not in stats:
            e = jnp.exp2(s - top)
            stats[b, h] = (
                top, jnp.sum(e, axis=0, keepdims=True), jnp.sum(e * dp, axis=0, keepdims=True)
            )
        else:
            m, l, w = stats[b, h]
            new = jnp.maximum(m, top)
            a = jnp.exp2(m - new)
            e = jnp.exp2(s - new)
            stats[b, h] = (
                new,
                l * a + jnp.sum(e, axis=0, keepdims=True),
                w * a + jnp.sum(e * dp, axis=0, keepdims=True),
            )

    def far_tiles(level):
        tiles = [(0, 0, 0), (1, 1, HEADS)]
        if level == 0:
            tiles.append((0, 1, 4 * HEADS))
        return tiles

    def key_tile(level, slot, qb, kb, h):
        sk[level, slot, h] = dot_nt(k[rows(kb), cols(h)], bbuf[level, 0, rows(qb), cols(h)]) * c2
        dpk[level, slot, h] = dot_nt(v[rows(kb), cols(h)], bbuf[level, 1, rows(qb), cols(h)])

    def query_level(level):
        for h in range(HEADS):
            if level == 0:
                query_tile(0, h, 1, fbuf[0, 0, rows(1), cols(h)], fbuf[0, 1, rows(1), cols(h)])
            for b in range(BPD):
                query_tile(
                    b, h, level + 2,
                    fbuf[level, 0, rows(b), cols(h)], fbuf[level, 1, rows(b), cols(h)],
                )

    def key_level(level):
        for slot, (qb, kb, _) in enumerate(far_tiles(level)):
            for h in range(HEADS):
                key_tile(level, slot, qb, kb, h)

    for h in range(HEADS):
        for b in range(BPD):
            query_tile(b, h, 0, k[rows(b), cols(h)], v[rows(b), cols(h)])
        query_tile(1, h, 1, k[rows(0), cols(h)], v[rows(0), cols(h)])

    for c in range(count):
        arrive(1, (c,))
        relay(1, (c,))
    query_level(1)
    key_level(1)
    arrive_front(0)
    query_level(0)
    for level in range(2, dists):
        for c in range(count):
            arrive_front(level, (c,))
            if level < dists - 1:
                arrive_back(level, (c,))
                relay(level, (c,))
        query_level(level)
        if level < dists - 1:
            key_level(level)

    final = {}
    for b in range(BPD):
        for h in range(HEADS):
            m, l, w = stats[b, h]
            final[b, h] = (m + jnp.log2(l), w / l)
    for level in range(dists):
        for b in range(BPD):
            for h in range(HEADS):
                lse, delta = final[b, h]
                row = b * HEADS + h
                sout[level, row : row + 1] = lse - bias(b, level + 2)
                row = row + BPD * HEADS
                sout[level, row : row + 1] = delta
                row = row + BPD * HEADS
                first = lse - bias(b, 1)
                sout[level, row : row + 1] = first

    def scopy(level, there):
        return pltpu.make_async_remote_copy(
            src_ref=sout.at[level],
            dst_ref=sin.at[level],
            send_sem=ssend.at[level],
            recv_sem=srecv.at[level],
            device_id={"ctx": there},
            device_id_type=MESH,
        )

    for level in range(dists - 1, -1, -1):

        @pl.when(me >= 2**level)
        def _():
            scopy(level, me - 2**level).start()

    arrive_back(0)
    key_level(0)
    arrive_back(dists - 1)
    key_level(dists - 1)

    dk_acc, dv_acc = {}, {}

    def add(acc, at, term):
        acc[at] = acc[at] + term if at in acc else term

    entries = bl.shape[1]
    for b in range(BPD):
        for h in range(HEADS):
            lse, delta = final[b, h]
            total = None
            for level in range(entries):
                p = jnp.exp2(sq[b, h, level] - lse)
                ds = (p * (dpq[b, h, level] - delta)).astype(BF16)
                if level == 0:
                    kb, local = k[rows(b), cols(h)], b
                elif level == 1 and b == 1:
                    kb, local = k[rows(0), cols(h)], 0
                elif level == 1:
                    kb, local = fbuf[0, 0, rows(1), cols(h)], None
                else:
                    kb, local = fbuf[level - 2, 0, rows(b), cols(h)], None
                term = dot_tn(ds, kb)
                total = term if total is None else total + term
                if local is not None:
                    add(dk_acc, (local, h), dot_nn(ds, q[rows(b), cols(h)]))
                    add(dv_acc, (local, h), dot_nn(p.astype(BF16), g[rows(b), cols(h)]))
            dq[rows(b), cols(h)] = (total * scale).astype(BF16)

    for level in range(dists):

        @pl.when(me + 2**level < n)
        def _():
            scopy(level, me + 2**level).wait_recv()

    for level in range(dists):
        for slot, (qb, kb, lse_row) in enumerate(far_tiles(level)):
            for h in range(HEADS):
                lse = sin[level, lse_row + h : lse_row + h + 1]
                at = (BPD + qb) * HEADS + h
                delta = sin[level, at : at + 1]
                p = jnp.exp2(sk[level, slot, h] - lse)
                ds = (p * (dpk[level, slot, h] - delta)).astype(BF16)
                add(dk_acc, (kb, h), dot_nn(ds, bbuf[level, 0, rows(qb), cols(h)]))
                add(dv_acc, (kb, h), dot_nn(p.astype(BF16), bbuf[level, 1, rows(qb), cols(h)]))
    for b in range(BPD):
        for h in range(HEADS):
            dk[rows(b), cols(h)] = (dk_acc[b, h] * scale).astype(BF16)
            dv[rows(b), cols(h)] = dv_acc[b, h].astype(BF16)

    for c in range(count):

        @pl.when(me + 2 < n)
        def _():
            fcopy(own_kv, 1, c, me + 2).wait_send()

        @pl.when(me >= 2)
        def _():
            bcopy(own_qg, 1, c, me - 2).wait_send()

        @pl.when(even)
        def _():
            fcopy(own_kv, 0, c, me + 1).wait_send()

            @pl.when(me + 2 < n)
            def _():
                bcopy(near_qg, 0, c, me + 1).wait_send()

        @pl.when(odd)
        def _():
            bcopy(own_qg, 0, c, me - 1).wait_send()

            @pl.when(me >= 2)
            def _():
                fcopy(near_kv, 0, c, me - 1).wait_send()

        for level in range(1, dists - 1):
            step = 2**level

            @pl.when((me >= step) & (me + step < n))
            def _():
                fcopy(held(fbuf, level), level + 1, c, me + step).wait_send()
                bcopy(held(bbuf, level), level + 1, c, me - step).wait_send()

    for level in range(dists):

        @pl.when(me >= 2**level)
        def _():
            scopy(level, me - 2**level).wait_send()


def store(a, b, c, a_out, b_out, c_out, sem):
    copies = [
        pltpu.make_async_copy(src, dst, sem.at[at])
        for at, (src, dst) in enumerate([(a, a_out), (b, b_out), (c, c_out)])
    ]
    for copy in copies:
        copy.start()
    for copy in copies:
        copy.wait()


def on_device(n, queries, keys, values, out_grad, block_list, causal):
    tok, feat = queries.shape
    entries = block_list.shape[1]
    dists = entries - 2
    d = feat // HEADS
    vmem = pl.BlockSpec(memory_space=pltpu.VMEM)
    hbm = pl.BlockSpec(memory_space=pltpu.HBM)
    chunks = 2 * BPD
    tile = (BLOCK, BLOCK)
    sems = pltpu.SemaphoreType.DMA((dists, chunks))
    out = jax.ShapeDtypeStruct((tok, feat), BF16)
    grads = pl.pallas_call(
        functools.partial(kernel, n, dists),
        out_shape=(out, out, out),
        in_specs=[hbm] * 6,
        out_specs=(vmem, vmem, vmem),
        scratch_shapes=[
            pltpu.SMEM(block_list.shape, jnp.int32),
            pltpu.SMEM(causal.shape, jnp.int32),
            *[pltpu.VMEM((tok, feat), BF16)] * 4,
            pltpu.VMEM((dists, 2, tok, feat), BF16),
            pltpu.VMEM((dists, 2, tok, feat), BF16),
            pltpu.VMEM((dists, 16, BLOCK), F32),
            pltpu.VMEM((dists, 16, BLOCK), F32),
            pltpu.VMEM((BPD, HEADS, entries) + tile, F32),
            pltpu.VMEM((BPD, HEADS, entries) + tile, F32),
            pltpu.VMEM((dists, 3, HEADS) + tile, F32),
            pltpu.VMEM((dists, 3, HEADS) + tile, F32),
            sems, sems, sems, sems,
            pltpu.SemaphoreType.DMA((dists,)),
            pltpu.SemaphoreType.DMA((dists,)),
            pltpu.SemaphoreType.DMA((6,)),
        ],
        compiler_params=pltpu.CompilerParams(
            collective_id=0, has_side_effects=True, vmem_limit_bytes=63 * 2**20
        ),
        cost_estimate=pl.CostEstimate(
            flops=128 * 2 * BLOCK * BLOCK * d, bytes_accessed=7 * tok * feat * 2,
            transcendentals=54 * BLOCK * BLOCK,
        ),
    )(block_list, causal, queries, keys, values, out_grad)
    return pl.pallas_call(
        store,
        out_shape=(out, out, out),
        in_specs=[vmem] * 3,
        out_specs=(hbm, hbm, hbm),
        scratch_shapes=[pltpu.SemaphoreType.DMA((3,))],
        cost_estimate=pl.CostEstimate(
            flops=0, bytes_accessed=3 * tok * feat * 2, transcendentals=0
        ),
    )(*grads)


def solution(mesh):
    rowspec = P(("dp", "ctx"), None)
    return jax.shard_map(
        functools.partial(on_device, mesh.shape["ctx"]),
        mesh=mesh,
        in_specs=(rowspec,) * 5 + (P(("dp", "ctx")),),
        out_specs=(rowspec,) * 3,
        check_vma=False,
    )
```
